256 devices in a mesh: row: 32 (over x, z), col: 8 (over y, core).
Axes of the slice: x: 4, y: 4, z: 8, core: 2. Of those that a mesh axis runs over, the one named last changes fastest.
Arguments:
- prev_factor: float32 [2, 1024, 32768], P(None, None, ('row', 'col')), may hold values from -0.03125 to 0.03125
- prev_solved: float32 [21, 32768], P(None, ('row', 'col')), may hold values from -6 to 6
- rhs: float32 [2, 21, 1024], replicated, may hold values from -6 to 6
- inverses: float32 [2, 1024, 1024], P(None, 'col'), may hold values from -1 to 2, as said below
- coupling: float32 [1024, 1024], P('col'), may hold values from -0.1875 to 0.1875
- trailing_factor: float32 [131072, 2, 1024], P('row', None, 'col'), may hold values from -0.125 to 0.125
- trailing_rhs: float32 [21, 131072], P(None, 'row'), may hold values from -6 to 6
Outputs:
- solved: float32 [2, 21, 1024], P(None, None, 'col')
- trailing_updated: float32 [21, 131072], P(None, 'row')
The draws below stay inside these ranges and needn't reach their ends.
Inputs may be any that keep to these rules, and one draw needn't show every extreme that they name: inverses[k] is lower triangular with a positive diagonal between 0.5 and 1.5.
All inputs are finite; a program needn't handle non-finite values.
Results may differ from the reference program's by a relative error of at most 0.000065.
Values sent between devices are 32-bit elements; how exact they have to be, the bound alone decides.
No kernel may reach another device: no remote copies, remote signals or barrier semaphores. Data moves between devices by JAX's collectives and lax.ppermute only.
A program may use at most 64 MiB of HBM per device.

```python
import math
import jax
import jax.numpy as jnp
from jax import lax

NB = 1024
R = 21
PREV = 32768
TRAIL = 131072


def draw_inverses(key, part):
    key = jax.random.fold_in(key, 7)
    first_key, second_key = jax.random.split(key)
    rows = lax.broadcasted_iota(jnp.int32, (2, NB, NB), 1)
    cols = lax.broadcasted_iota(jnp.int32, (2, NB, NB), 2)
    diag = jax.random.uniform(first_key, (2, NB, NB), jnp.float32, 0.75, 1.25)
    lower = jnp.clip(jax.random.normal(second_key, (2, NB, NB), jnp.float32), -2.5, 2.5) * (0.4 / math.sqrt(NB))
    return jnp.where(rows == cols, diag, jnp.where(rows > cols, lower, 0.0))


def block_scale(own_key, dims, pieces, least, top_value):
    level, own = 1.0, jax.random.fold_in(own_key, 6)
    for position, parts in pieces:
        heights = jnp.exp(jax.random.uniform(jax.random.fold_in(own, position), (parts,), jnp.float32, least / len(pieces), top_value / len(pieces)))
        level = level * jnp.repeat(heights, dims[position] // parts).reshape([-1 if axis == position else 1 for axis in range(len(dims))])
    return level


def centred(key, dims, scale, limit, shards=(), dtype=jnp.bfloat16):
    array = scale * jax.random.normal(key, dims, jnp.float32)
    if shards:
        array = array * block_scale(key, dims, shards, -0.22, 0.18)
    return jnp.clip(array, -limit, limit).astype(dtype)


def setup_inputs(seed: int = 0) -> dict:
    key_list = jax.random.split(jax.random.key(seed), 8)
    return {
        "prev_factor": centred(key_list[0], (2, NB, PREV), PREV ** -0.5, 0.03125, ((2, 256),), jnp.float32),
        "prev_solved": centred(key_list[1], (R, PREV), 1.0, 6.0, ((1, 256),), jnp.float32),
        "rhs": centred(key_list[2], (2, R, NB), 1.0, 6.0, (), jnp.float32),
        "inverses": draw_inverses(jax.random.fold_in(key_list[7], 71), 0),
        "coupling": centred(key_list[4], (NB, NB), NB ** -0.5, 0.1875, ((0, 8),), jnp.float32),
        "trailing_factor": centred(key_list[5], (TRAIL, 2, NB), (2 * NB) ** -0.5, 0.125, ((0, 32), (2, 8)), jnp.float32),
        "trailing_rhs": centred(key_list[6], (R, TRAIL), 1.0, 6.0, ((1, 32),), jnp.float32),
    }


def reference(prev_factor, prev_solved, rhs, inverses, coupling, trailing_factor, trailing_rhs):
    highest = lax.Precision.HIGHEST
    partial_value = jnp.einsum('kip,rp->kri', prev_factor, prev_solved, precision=highest)
    first = rhs[0] - partial_value[0]
    block0 = jnp.einsum('ij,rj->ri', inverses[0], first, precision=highest)
    second = rhs[1] - partial_value[1] - jnp.einsum('ij,rj->ri', coupling, block0, precision=highest)
    block1 = jnp.einsum('ij,rj->ri', inverses[1], second, precision=highest)
    solved = jnp.stack([block0, block1])
    trailing_updated = trailing_rhs - jnp.einsum('tkj,krj->rt', trailing_factor, solved, precision=highest)
    return solved, trailing_updated
```

```python
import jax
import jax.numpy as jnp
from jax import lax
from jax.sharding import PartitionSpec as P

HIGH = lax.Precision.HIGH


def local(prev_factor, prev_solved, rhs, inverses, coupling, trailing_factor, trailing_rhs):
    width = inverses.shape[1]
    row, col = lax.axis_index("row"), lax.axis_index("col")
    core, y = col % 2, col // 2

    def swap(value, axis, mask):
        size = lax.axis_size(axis)
        return lax.ppermute(value, axis, [(i, i ^ mask) for i in range(size)])

    def col_sum(value):
        for mask in (1, 2, 6):
            value = value + swap(value, "col", mask)
        return value

    blocks = coupling.reshape(width, 4, 2, width)
    kept = lax.dynamic_index_in_dim(blocks, core, 2, keepdims=False)
    given = lax.dynamic_index_in_dim(blocks, 1 - core, 2, keepdims=False)
    taken = swap(given, "col", 1)
    pair = jnp.where(core == 0, jnp.concatenate([kept, taken]), jnp.concatenate([taken, kept]))
    columns = jnp.zeros((4, 2 * width, width), jnp.float32)
    for mask in range(4):
        block = lax.dynamic_index_in_dim(pair, y ^ mask, 1, keepdims=False)
        if mask:
            block = swap(block, "col", 2 * mask)
        columns = lax.dynamic_update_index_in_dim(columns, block, y ^ mask, 0)
    columns = columns.reshape(8 * width, width)

    partial0 = jnp.einsum("ip,rp->ri", prev_factor[0], prev_solved, precision=HIGH)
    partial1 = jnp.einsum("ip,rp->ri", prev_factor[1], prev_solved, precision=HIGH)
    first = jnp.where(row == 0, rhs[0], 0.0) - col_sum(partial0)
    block0 = jnp.einsum("ij,rj->ri", inverses[0], first, precision=HIGH)
    own1 = jnp.where((row == 0) & (col == 0), rhs[1], 0.0) - partial1
    second = col_sum(own1 - jnp.einsum("ij,rj->ri", columns, block0, precision=HIGH))
    block1 = jnp.einsum("ij,rj->ri", inverses[1], second, precision=HIGH)

    solved = jnp.stack([block0, block1])
    solved = solved + swap(solved, "row", 8)
    solved = solved + swap(solved, "row", 24)
    groups = [[8 * x + z for z in range(8)] for x in range(4)]
    copies = jnp.broadcast_to(solved[None], (8, *solved.shape))
    solved = jnp.sum(lax.all_to_all(copies, "row", 0, 0, axis_index_groups=groups), axis=0)

    products = jnp.einsum("tkj,krj->rt", trailing_factor, solved, precision=HIGH)
    half = products.shape[1] // 2
    mine = lax.dynamic_slice_in_dim(products, core * half, half, 1)
    other = lax.dynamic_slice_in_dim(products, (1 - core) * half, half, 1)
    mine = mine + swap(other, "col", 1)
    mine = mine + swap(mine, "col", 2)
    mine = mine + swap(mine, "col", 6)
    mine = lax.dynamic_slice_in_dim(trailing_rhs, core * half, half, 1) - mine
    other = swap(mine, "col", 1)
    updated = jnp.where(core == 0, jnp.concatenate([mine, other], 1), jnp.concatenate([other, mine], 1))
    return (solved, updated)


def solution(mesh):
    in_specs = (
        P(None, None, ("row", "col")),
        P(None, ("row", "col")),
        P(),
        P(None, "col", None),
        P("col", None),
        P("row", None, "col"),
        P(None, "row"),
    )
    out_specs = (P(None, None, "col"), P(None, "row"))
    return jax.shard_map(local, mesh=mesh, in_specs=in_specs, out_specs=out_specs, check_vma=False)
```

```python
import jax
import jax.numpy as jnp
from jax import lax
from jax.experimental import pallas as pl
from jax.experimental.pallas import tpu as pltpu
from jax.sharding import PartitionSpec as P

HIGH = lax.Precision.HIGH
CHUNKS = 2
NT = (((1,), (1,)), ((), ()))


def head_and_tail(value):
    head = value.astype(jnp.bfloat16)
    return head, (value - head.astype(jnp.float32)).astype(jnp.bfloat16)


def trailing_kernel(core_ref, solved_ref, factor_ref, other_ref, mine_ref):
    solved = solved_ref[...]
    rhs, count = mine_ref.shape
    pad = -rhs % 8
    solved = jnp.concatenate([solved[:rhs], solved[rhs:]], 1)
    solved = jnp.concatenate([solved, jnp.zeros((pad, solved.shape[1]), jnp.float32)], 0)
    head = solved.astype(jnp.bfloat16).astype(jnp.float32)
    both = jnp.concatenate([head, solved - head], 0).astype(jnp.bfloat16)
    head = head.astype(jnp.bfloat16)
    size = count // CHUNKS
    for out_ref, half in ((other_ref, 1 - core_ref[0]), (mine_ref, core_ref[0])):
        start = pl.multiple_of(2 * count * half, 2 * count)
        for i in range(CHUNKS):
            block = [factor_ref[pl.ds(start + 2 * size * i + k, size, 2), :] for k in range(2)]
            heads, tails = head_and_tail(jnp.concatenate(block, 1))
            main = lax.dot_general(both, heads, NT, preferred_element_type=jnp.float32)
            side = lax.dot_general(head, tails, NT, preferred_element_type=jnp.float32)
            out_ref[:, size * i : size * (i + 1)] = main[:rhs] + (main[rhs + pad : 2 * rhs + pad] + side[:rhs])


def trailing_products(factor, solved, core):
    count, rhs, width = factor.shape[0] // 4, solved.shape[0] // 2, factor.shape[1]
    vmem = pl.BlockSpec(memory_space=pltpu.VMEM)
    return pl.pallas_call(
        trailing_kernel,
        in_specs=[pl.BlockSpec(memory_space=pltpu.SMEM), vmem, vmem],
        out_specs=[vmem] * 2,
        out_shape=[jax.ShapeDtypeStruct((rhs, count), jnp.float32)] * 2,
        cost_estimate=pl.CostEstimate(flops=24 * count * width * rhs, bytes_accessed=16 * count * width, transcendentals=0),
        compiler_params=pltpu.CompilerParams(vmem_limit_bytes=8 * 2**20),
    )(core.reshape(1), solved, pltpu.with_memory_space_constraint(factor, pltpu.VMEM))


def local(prev_factor, prev_solved, rhs, inverses, coupling, trailing_factor, trailing_rhs):
    width = inverses.shape[1]
    row, col = lax.axis_index("row"), lax.axis_index("col")
    core, y = col % 2, col // 2
    both = ("row", "col")

    def swap(value, mask0, mask1=None):
        masks = (mask0, mask0 if mask1 is None else mask1)
        return lax.ppermute(value, both, [(i, i ^ masks[i % 2]) for i in range(256)])

    def y_sum(value):
        value = value + swap(value, 2, 6)
        return value + swap(value, 6, 2)

    def lanes(value, start, size):
        return lax.dynamic_slice_in_dim(value, start, size, value.ndim - 1)

    def by_core(mine, other):
        return jnp.where(core == 0, mine, other), jnp.where(core == 0, other, mine)

    def dot(matrix, value):
        return jnp.einsum("ij,rj->ri", matrix, value, precision=HIGH)

    def among_leaders(value, step):
        return [swap(value, mask, step * i) for i, mask in ((1, 2), (2, 64), (3, 8))]

    def quad_sum(value, step):
        one, two, three = among_leaders(value, step)
        return (value + one) + (two + three)

    def here(value):
        return lax.optimization_barrier(jnp.where(core >= 0, value, 0.0))

    def both_rows(other, mine, value):
        return jnp.concatenate([dot(other, value), dot(mine, value)], 1)

    def gathered(value):
        one, two, three = among_leaders(value, 2)
        return jnp.concatenate(
            [
                jnp.where(y == i, value, jnp.where(y == i ^ 1, one, jnp.where(y == i ^ 2, two, three)))
                for i in range(4)
            ],
            1,
        )

    given = dot(lax.dynamic_index_in_dim(prev_factor, core, 0, keepdims=False), prev_solved)
    taken = swap(given, 1)
    kept = dot(lax.dynamic_index_in_dim(prev_factor, 1 - core, 0, keepdims=False), prev_solved)
    kept = lax.optimization_barrier(kept)
    sums, inverses, coupling, rhs = lax.optimization_barrier((kept + taken, inverses, coupling, rhs))
    other_inverses, other_coupling = swap(inverses, 1), here(swap(coupling, 1))
    other_inverses = here(other_inverses[0]), here(other_inverses[1])
    start = jnp.where(row == 0, lax.dynamic_index_in_dim(rhs, 1 - core, 0, keepdims=False), 0.0)
    reduced = start - y_sum(sums)
    own1 = swap(lanes(reduced, 2 * width * y, 2 * width), 1)
    block0 = both_rows(other_inverses[0], here(inverses[0]), reduced)
    second = own1 - both_rows(other_coupling, coupling, gathered(block0))
    block1 = both_rows(other_inverses[1], inverses[1], gathered(second))

    solved = quad_sum(quad_sum(jnp.concatenate([block0, block1]), 64), 8)
    solved = solved + swap(solved, 2, 56)
    other = swap(solved[:, :width], 1)
    solved = jnp.where(core == 0, other, solved[:, width:])
    other, mine = trailing_products(trailing_factor.reshape(-1, width), solved, core)
    mine = y_sum(mine + swap(other, 1))
    half = mine.shape[1]
    mine = lanes(trailing_rhs, core * half, half) - mine
    return (solved.reshape(2, -1, width), jnp.concatenate(by_core(mine, swap(mine, 1)), 1))


def solution(mesh):
    in_specs = (
        P(None, None, ("row", "col")),
        P(None, ("row", "col")),
        P(),
        P(None, "col", None),
        P("col", None),
        P("row", None, "col"),
        P(None, "row"),
    )
    out_specs = (P(None, None, "col"), P(None, "row"))
    return jax.shard_map(local, mesh=mesh, in_specs=in_specs, out_specs=out_specs, check_vma=False)
```

```python
import jax
import jax.numpy as jnp
from jax import lax
from jax.experimental import pallas as pl
from jax.experimental.pallas import tpu as pltpu
from jax.sharding import PartitionSpec as P

HIGH = lax.Precision.HIGH
CHUNKS = 2
NT = (((1,), (1,)), ((), ()))


def head_and_tail(value):
    head = value.astype(jnp.bfloat16)
    return head, (value - head.astype(jnp.float32)).astype(jnp.bfloat16)


def product(left, right):
    rows, pad = left.shape[0], -left.shape[0] % 8
    left = jnp.concatenate([left, jnp.zeros((pad, left.shape[1]), jnp.float32)], 0)
    head = left.astype(jnp.bfloat16).astype(jnp.float32)
    both = jnp.concatenate([head, left - head], 0).astype(jnp.bfloat16)
    heads, tails = head_and_tail(right)
    main = lax.dot_general(both, heads, NT, preferred_element_type=jnp.float32)
    side = lax.dot_general(head.astype(jnp.bfloat16), tails, NT, preferred_element_type=jnp.float32)
    return main[:rows] + (main[rows + pad : 2 * rows + pad] + side[:rows])


def local_call(kernel, out_shape, scalar, *arrays, pinned=(), work=(0, 0)):
    vmem = pl.BlockSpec(memory_space=pltpu.VMEM)
    pinned = [pltpu.with_memory_space_constraint(array, pltpu.VMEM) for array in pinned]
    return pl.pallas_call(
        kernel,
        in_specs=[pl.BlockSpec(memory_space=pltpu.SMEM)] + [vmem] * (len(arrays) + len(pinned)),
        out_specs=[vmem] * len(out_shape),
        out_shape=[jax.ShapeDtypeStruct(shape, jnp.float32) for shape in out_shape],
        cost_estimate=pl.CostEstimate(flops=work[0], bytes_accessed=work[1], transcendentals=0),
        compiler_params=pltpu.CompilerParams(vmem_limit_bytes=8 * 2**20),
    )(scalar.reshape(1), *arrays, *pinned)


def rows_of_both(other_ref, own_ref):
    return jnp.concatenate([other_ref[...], own_ref[...]], 0)


def in_order(y, refs):
    own, one, two, three = [ref[...] for ref in refs]
    blocks = [jnp.where(y == i, own, jnp.where(y == i ^ 1, one, jnp.where(y == i ^ 2, two, three))) for i in range(4)]
    return jnp.concatenate(blocks, 1)


def first_kernel(y_ref, reduced_ref, other_ref, own_ref, out_ref):
    out_ref[...] = product(reduced_ref[...], rows_of_both(other_ref, own_ref))


def second_kernel(y_ref, base_ref, own0, one0, two0, three0, other_ref, own_ref, out_ref):
    known = in_order(y_ref[0], (own0, one0, two0, three0))
    out_ref[...] = base_ref[...] - product(known, rows_of_both(other_ref, own_ref))


def third_kernel(y_ref, block0_ref, own1, one1, two1, three1, other_ref, own_ref, out_ref):
    known = in_order(y_ref[0], (own1, one1, two1, three1))
    rows = block0_ref.shape[0]
    out_ref[:rows, :] = block0_ref[...]
    out_ref[rows:, :] = product(known, rows_of_both(other_ref, own_ref))


def unknowns(core_ref, leader_ref, taken_ref):
    return jnp.where(core_ref[0] == 0, taken_ref[...], leader_ref[:, taken_ref.shape[1] :])


def trailing_kernel(own, core_ref, leader_ref, taken_ref, factor_ref, out_ref, *solved_ref):
    solved = unknowns(core_ref, leader_ref, taken_ref)
    if own:
        solved_ref[0][...] = solved
    rhs, count = out_ref.shape
    pad = -rhs % 8
    solved = jnp.concatenate([solved[:rhs], solved[rhs:]], 1)
    solved = jnp.concatenate([solved, jnp.zeros((pad, solved.shape[1]), jnp.float32)], 0)
    head = solved.astype(jnp.bfloat16).astype(jnp.float32)
    both = jnp.concatenate([head, solved - head], 0).astype(jnp.bfloat16)
    head = head.astype(jnp.bfloat16)
    size = count // CHUNKS
    start = pl.multiple_of(2 * count * (core_ref[0] if own else 1 - core_ref[0]), 2 * count)
    for i in range(CHUNKS):
        block = [factor_ref[pl.ds(start + 2 * size * i + k, size, 2), :] for k in range(2)]
        heads, tails = head_and_tail(jnp.concatenate(block, 1))
        main = lax.dot_general(both, heads, NT, preferred_element_type=jnp.float32)
        side = lax.dot_general(head, tails, NT, preferred_element_type=jnp.float32)
        out_ref[:, size * i : size * (i + 1)] = main[:rhs] + (main[rhs + pad : 2 * rhs + pad] + side[:rhs])


def trailing_products(own, factor, leader, taken, core):
    count, rhs, width = factor.shape[0] // 4, taken.shape[0] // 2, factor.shape[1]
    vmem = pl.BlockSpec(memory_space=pltpu.VMEM)
    out_shape = [jax.ShapeDtypeStruct((rhs, count), jnp.float32)]
    if own:
        out_shape.append(jax.ShapeDtypeStruct(taken.shape, jnp.float32))
    return pl.pallas_call(
        lambda *refs: trailing_kernel(own, *refs),
        in_specs=[pl.BlockSpec(memory_space=pltpu.SMEM), vmem, vmem, vmem],
        out_specs=[vmem] * len(out_shape),
        out_shape=out_shape,
        cost_estimate=pl.CostEstimate(flops=12 * count * width * rhs, bytes_accessed=8 * count * width, transcendentals=0),
        compiler_params=pltpu.CompilerParams(vmem_limit_bytes=8 * 2**20),
    )(core.reshape(1), leader, taken, pltpu.with_memory_space_constraint(factor, pltpu.VMEM))


def place_kernel(half_ref, value_ref, *rest):
    out_ref, sem = rest[-2:]
    count = value_ref.shape[1]
    start = pl.multiple_of(half_ref[0] * count, count)
    copy = pltpu.make_async_copy(value_ref, out_ref.at[:, pl.ds(start, count)], sem)
    copy.start()
    copy.wait()


def place(half, value, *target):
    vmem, anywhere = pl.BlockSpec(memory_space=pltpu.VMEM), pl.BlockSpec(memory_space=pl.ANY)
    return pl.pallas_call(
        place_kernel,
        in_specs=[pl.BlockSpec(memory_space=pltpu.SMEM), vmem] + [anywhere] * len(target),
        out_specs=anywhere,
        out_shape=jax.ShapeDtypeStruct((value.shape[0], 2 * value.shape[1]), jnp.float32),
        scratch_shapes=[pltpu.SemaphoreType.DMA],
        input_output_aliases={2: 0} if target else {},
    )(half.reshape(1), pltpu.with_memory_space_constraint(value, pltpu.VMEM), *target)


def local(prev_factor, prev_solved, rhs, inverses, coupling, trailing_factor, trailing_rhs):
    width = inverses.shape[1]
    row, col = lax.axis_index("row"), lax.axis_index("col")
    core, y = col & 1, col >> 1
    both = ("row", "col")

    def swap(value, mask0, mask1=None):
        masks = (mask0, mask0 if mask1 is None else mask1)
        return lax.ppermute(value, both, [(i, i ^ masks[i % 2]) for i in range(256)])

    def y_sum(value):
        value = value + swap(value, 2, 6)
        return value + swap(value, 6, 2)

    def lanes(value, start, size):
        return lax.dynamic_slice_in_dim(value, start, size, value.ndim - 1)

    def by_core(mine, other):
        return jnp.where(core == 0, mine, other), jnp.where(core == 0, other, mine)

    def dot(matrix, value):
        return jnp.einsum("ij,rj->ri", matrix, value, precision=HIGH)

    def among_leaders(value, step):
        return [swap(value, mask, step * i) for i, mask in ((1, 2), (2, 64), (3, 8))]

    def quad_sum(value, step):
        one, two, three = among_leaders(value, step)
        return (value + one) + (two + three)

    def here(value):
        return lax.optimization_barrier(jnp.where(core >= 0, value, 0.0))

    given = dot(lax.dynamic_index_in_dim(prev_factor, core, 0, keepdims=False), prev_solved)
    taken = swap(given, 1)
    kept = dot(lax.dynamic_index_in_dim(prev_factor, 1 - core, 0, keepdims=False), prev_solved)
    kept = lax.optimization_barrier(kept)
    sums, inverses, coupling, rhs = lax.optimization_barrier((kept + taken, inverses, coupling, rhs))
    other_inverses = swap(inverses, 1)
    inverses0 = here(other_inverses[0]), here(inverses[0])
    inverses1 = here(other_inverses[1]), here(inverses[1])
    one, two, three = swap(sums, 2, 6), swap(sums, 6, 2), swap(sums, 4)
    one, coupling = lax.optimization_barrier((one, coupling))
    couplings = here(swap(coupling, 1)), here(coupling)
    start = jnp.where(row == 0, lax.dynamic_index_in_dim(rhs, 1 - core, 0, keepdims=False), 0.0)
    reduced = start - ((sums + one) + (two + three))
    rows, work = reduced.shape[0], (12 * 21 * width * 8 * width, 16 * width * 8 * width)
    shape = (rows, 2 * width)
    (block0,) = local_call(first_kernel, [shape], y, reduced, pinned=inverses0, work=work)
    block0, own1 = lax.optimization_barrier((block0, lanes(reduced, 2 * width * y, 2 * width)))
    others = among_leaders(block0, 2)
    (second,) = local_call(second_kernel, [shape], y, swap(own1, 1), block0, *others, pinned=couplings, work=work)
    others = among_leaders(second, 2)
    (solved,) = local_call(third_kernel, [(2 * rows, 2 * width)], y, block0, second, *others, pinned=inverses1, work=work)
    solved = quad_sum(solved, 64)
    solved, trailing_factor = lax.optimization_barrier((solved, trailing_factor))
    solved = quad_sum(solved, 8)
    solved = solved + swap(solved, 2, 48)
    taken = swap(solved[:, :width], 1)

    factor = trailing_factor.reshape(-1, width)
    (other,) = trailing_products(False, factor, solved, taken, core)
    mine, solved = trailing_products(True, factor, solved, taken, core)
    mine = y_sum(mine + swap(other, 1))
    half = mine.shape[1]
    mine = lanes(trailing_rhs, core * half, half) - mine
    updated = place(1 - core, swap(mine, 1), place(core, mine))
    return (solved.reshape(2, -1, width), updated)


def solution(mesh):
    in_specs = (
        P(None, None, ("row", "col")),
        P(None, ("row", "col")),
        P(),
        P(None, "col", None),
        P("col", None),
        P("row", None, "col"),
        P(None, "row"),
    )
    out_specs = (P(None, None, "col"), P(None, "row"))
    return jax.shard_map(local, mesh=mesh, in_specs=in_specs, out_specs=out_specs, check_vma=False)
```

```python
import jax
import jax.numpy as jnp
from jax import lax
from jax.experimental import pallas as pl
from jax.experimental.pallas import tpu as pltpu
from jax.sharding import PartitionSpec as P

HIGH = lax.Precision.HIGH
CHUNKS = 2
NT = (((1,), (1,)), ((), ()))


def head_and_tail(value):
    head = value.astype(jnp.bfloat16)
    return head, (value - head.astype(jnp.float32)).astype(jnp.bfloat16)


def product(left, right):
    rows, pad = left.shape[0], -left.shape[0] % 8
    left = jnp.concatenate([left, jnp.zeros((pad, left.shape[1]), jnp.float32)], 0)
    head = left.astype(jnp.bfloat16).astype(jnp.float32)
    both = jnp.concatenate([head, left - head], 0).astype(jnp.bfloat16)
    heads, tails = head_and_tail(right)
    main = lax.dot_general(both, heads, NT, preferred_element_type=jnp.float32)
    side = lax.dot_general(head.astype(jnp.bfloat16), tails, NT, preferred_element_type=jnp.float32)
    return main[:rows] + (main[rows + pad : 2 * rows + pad] + side[:rows])


def local_call(kernel, out_shape, scalar, *arrays, pinned=(), work=(0, 0)):
    vmem = pl.BlockSpec(memory_space=pltpu.VMEM)
    pinned = [pltpu.with_memory_space_constraint(array, pltpu.VMEM) for array in pinned]
    return pl.pallas_call(
        kernel,
        in_specs=[pl.BlockSpec(memory_space=pltpu.SMEM)] + [vmem] * (len(arrays) + len(pinned)),
        out_specs=[vmem] * len(out_shape),
        out_shape=[jax.ShapeDtypeStruct(shape, jnp.float32) for shape in out_shape],
        cost_estimate=pl.CostEstimate(flops=work[0], bytes_accessed=work[1], transcendentals=0),
        compiler_params=pltpu.CompilerParams(vmem_limit_bytes=8 * 2**20),
    )(scalar.reshape(1), *arrays, *pinned)


def rows_of_both(other_ref, own_ref):
    return jnp.concatenate([other_ref[...], own_ref[...]], 0)


def in_order(y, refs):
    own, two, three, one = [ref[...] for ref in refs]
    blocks = [jnp.where(y == i, own, jnp.where(y == i ^ 1, one, jnp.where(y == i ^ 2, two, three))) for i in range(4)]
    return jnp.concatenate(blocks, 1)


def first_kernel(y_ref, reduced_ref, other_ref, own_ref, out_ref):
    out_ref[...] = product(reduced_ref[...], rows_of_both(other_ref, own_ref))


def second_kernel(y_ref, base_ref, own0, two0, three0, one0, other_ref, own_ref, out_ref):
    known = in_order(y_ref[0], (own0, two0, three0, one0))
    out_ref[...] = base_ref[...] - product(known, rows_of_both(other_ref, own_ref))


def third_kernel(y_ref, block0_ref, own1, two1, three1, one1, other_ref, own_ref, out_ref):
    known = in_order(y_ref[0], (own1, two1, three1, one1))
    rows = block0_ref.shape[0]
    out_ref[:rows, :] = block0_ref[...]
    out_ref[rows:, :] = product(known, rows_of_both(other_ref, own_ref))


def unknowns(core_ref, leader_ref, taken_ref):
    return jnp.where(core_ref[0] == 0, taken_ref[...], leader_ref[:, taken_ref.shape[1] :])


def trailing_kernel(own, core_ref, leader_ref, taken_ref, factor_ref, out_ref, *solved_ref):
    solved = unknowns(core_ref, leader_ref, taken_ref)
    if own:
        solved_ref[0][...] = solved
    rhs, count = out_ref.shape
    pad = -rhs % 8
    solved = jnp.concatenate([solved[:rhs], solved[rhs:]], 1)
    solved = jnp.concatenate([solved, jnp.zeros((pad, solved.shape[1]), jnp.float32)], 0)
    head = solved.astype(jnp.bfloat16).astype(jnp.float32)
    both = jnp.concatenate([head, solved - head], 0).astype(jnp.bfloat16)
    head = head.astype(jnp.bfloat16)
    size = count // CHUNKS
    start = pl.multiple_of(2 * count * (core_ref[0] if own else 1 - core_ref[0]), 2 * count)
    for i in range(CHUNKS):
        block = [factor_ref[pl.ds(start + 2 * size * i + k, size, 2), :] for k in range(2)]
        heads, tails = head_and_tail(jnp.concatenate(block, 1))
        main = lax.dot_general(both, heads, NT, preferred_element_type=jnp.float32)
        side = lax.dot_general(head, tails, NT, preferred_element_type=jnp.float32)
        out_ref[:, size * i : size * (i + 1)] = main[:rhs] + (main[rhs + pad : 2 * rhs + pad] + side[:rhs])


def trailing_products(own, factor, leader, taken, core):
    count, rhs, width = factor.shape[0] // 4, taken.shape[0] // 2, factor.shape[1]
    vmem = pl.BlockSpec(memory_space=pltpu.VMEM)
    out_shape = [jax.ShapeDtypeStruct((rhs, count), jnp.float32)]
    if own:
        out_shape.append(jax.ShapeDtypeStruct(taken.shape, jnp.float32))
    return pl.pallas_call(
        lambda *refs: trailing_kernel(own, *refs),
        in_specs=[pl.BlockSpec(memory_space=pltpu.SMEM), vmem, vmem, vmem],
        out_specs=[vmem] * len(out_shape),
        out_shape=out_shape,
        cost_estimate=pl.CostEstimate(flops=12 * count * width * rhs, bytes_accessed=8 * count * width, transcendentals=0),
        compiler_params=pltpu.CompilerParams(vmem_limit_bytes=8 * 2**20),
    )(core.reshape(1), leader, taken, pltpu.with_memory_space_constraint(factor, pltpu.VMEM))


def place_kernel(half_ref, value_ref, *rest):
    out_ref, sem = rest[-2:]
    count = value_ref.shape[1]
    start = pl.multiple_of(half_ref[0] * count, count)
    copy = pltpu.make_async_copy(value_ref, out_ref.at[:, pl.ds(start, count)], sem)
    copy.start()
    copy.wait()


def place(half, value, *target):
    vmem, anywhere = pl.BlockSpec(memory_space=pltpu.VMEM), pl.BlockSpec(memory_space=pl.ANY)
    return pl.pallas_call(
        place_kernel,
        in_specs=[pl.BlockSpec(memory_space=pltpu.SMEM), vmem] + [anywhere] * len(target),
        out_specs=anywhere,
        out_shape=jax.ShapeDtypeStruct((value.shape[0], 2 * value.shape[1]), jnp.float32),
        scratch_shapes=[pltpu.SemaphoreType.DMA],
        input_output_aliases={2: 0} if target else {},
    )(half.reshape(1), pltpu.with_memory_space_constraint(value, pltpu.VMEM), *target)


def local(prev_factor, prev_solved, rhs, inverses, coupling, trailing_factor, trailing_rhs):
    width = inverses.shape[1]
    row, col = lax.axis_index("row"), lax.axis_index("col")
    core, y = col & 1, col >> 1
    both = ("row", "col")

    def swap(value, mask0, mask1=None):
        masks = (mask0, mask0 if mask1 is None else mask1)
        return lax.ppermute(value, both, [(i, i ^ masks[i % 2]) for i in range(256)])

    def y_sum(value):
        value = value + swap(value, 2, 6)
        return value + swap(value, 6, 2)

    def lanes(value, start, size):
        return lax.dynamic_slice_in_dim(value, start, size, value.ndim - 1)

    def by_core(mine, other):
        return jnp.where(core == 0, mine, other), jnp.where(core == 0, other, mine)

    def dot(matrix, value):
        return jnp.einsum("ij,rj->ri", matrix, value, precision=HIGH)

    def among_leaders(value, step, mask):
        return [swap(value, mask, step * i) for i in (2, 3, 1)]

    def from_z(value, source):
        pairs = [(i, i ^ 2) for i in range(0, 256, 2)]
        pairs += [((i & ~56) | source(i >> 3 & 7) << 3, i) for i in range(1, 256, 2)]
        return lax.ppermute(value, both, pairs)

    def z_sum(value):
        value = value + swap(value, 2, 8)
        beside = from_z(value, lambda z: (z + 1 if z & 1 else z - 1) & 7)
        beyond = from_z(value, lambda z: (z - 2 if z & 1 else z + 2) & 7)
        opposite = from_z(value, lambda z: z ^ 5)
        return (value + opposite) + (beyond + beside)

    def here(value):
        return lax.optimization_barrier(jnp.where(core >= 0, value, 0.0))

    given = dot(lax.dynamic_index_in_dim(prev_factor, core, 0, keepdims=False), prev_solved)
    taken = swap(given, 1)
    kept = dot(lax.dynamic_index_in_dim(prev_factor, 1 - core, 0, keepdims=False), prev_solved)
    kept = lax.optimization_barrier(kept)
    sums, inverses, coupling, rhs = lax.optimization_barrier((kept + taken, inverses, coupling, rhs))
    other_inverses = swap(inverses, 1)
    inverses0 = here(other_inverses[0]), here(inverses[0])
    inverses1 = here(other_inverses[1]), here(inverses[1])
    one, two, three = swap(sums, 2, 6), swap(sums, 6, 2), swap(sums, 4)
    one, coupling = lax.optimization_barrier((one, coupling))
    couplings = here(swap(coupling, 1)), here(coupling)
    start = jnp.where(row == 0, lax.dynamic_index_in_dim(rhs, 1 - core, 0, keepdims=False), 0.0)
    reduced = start - ((three + two) + (one + sums))
    rows, work = reduced.shape[0], (12 * 21 * width * 8 * width, 16 * width * 8 * width)
    shape = (rows, 2 * width)
    (block0,) = local_call(first_kernel, [shape], y, reduced, pinned=inverses0, work=work)
    block0, own1 = lax.optimization_barrier((block0, lanes(reduced, 2 * width * y, 2 * width)))
    others = among_leaders(block0, 2, 64)
    (second,) = local_call(second_kernel, [shape], y, swap(own1, 1), block0, *others, pinned=couplings, work=work)
    others = among_leaders(second, 2, 64)
    (solved,) = local_call(third_kernel, [(2 * rows, 2 * width)], y, block0, second, *others, pinned=inverses1, work=work)
    two, three, one = among_leaders(solved, 64, 2)
    solved = (two + three) + (one + solved)
    solved, trailing_factor = lax.optimization_barrier((solved, trailing_factor))
    solved = z_sum(solved)
    taken = swap(solved[:, :width], 1)

    factor = trailing_factor.reshape(-1, width)
    (other,) = trailing_products(False, factor, solved, taken, core)
    mine, solved = trailing_products(True, factor, solved, taken, core)
    mine = y_sum(mine + swap(other, 1))
    half = mine.shape[1]
    mine = lanes(trailing_rhs, core * half, half) - mine
    updated = place(1 - core, swap(mine, 1), place(core, mine))
    return (solved.reshape(2, -1, width), updated)


def solution(mesh):
    in_specs = (
        P(None, None, ("row", "col")),
        P(None, ("row", "col")),
        P(),
        P(None, "col", None),
        P("col", None),
        P("row", None, "col"),
        P(None, "row"),
    )
    out_specs = (P(None, None, "col"), P(None, "row"))
    return jax.shard_map(local, mesh=mesh, in_specs=in_specs, out_specs=out_specs, check_vma=False)
```

```python
import jax
import jax.numpy as jnp
from jax import lax
from jax.experimental import pallas as pl
from jax.experimental.pallas import tpu as pltpu
from jax.sharding import PartitionSpec as P

HIGH = lax.Precision.HIGH
CHUNKS = 2
NT = (((1,), (1,)), ((), ()))


def head_and_tail(value):
    head = value.astype(jnp.bfloat16)
    return head, (value - head.astype(jnp.float32)).astype(jnp.bfloat16)


def product(left, right):
    rows, pad = left.shape[0], -left.shape[0] % 8
    left = jnp.concatenate([left, jnp.zeros((pad, left.shape[1]), jnp.float32)], 0)
    head = left.astype(jnp.bfloat16).astype(jnp.float32)
    both = jnp.concatenate([head, left - head], 0).astype(jnp.bfloat16)
    heads, tails = head_and_tail(right)
    main = lax.dot_general(both, heads, NT, preferred_element_type=jnp.float32)
    side = lax.dot_general(head.astype(jnp.bfloat16), tails, NT, preferred_element_type=jnp.float32)
    return main[:rows] + (main[rows + pad : 2 * rows + pad] + side[:rows])


def local_call(kernel, out_shape, scalar, *arrays, pinned=(), work=(0, 0)):
    vmem = pl.BlockSpec(memory_space=pltpu.VMEM)
    pinned = [pltpu.with_memory_space_constraint(array, pltpu.VMEM) for array in pinned]
    return pl.pallas_call(
        kernel,
        in_specs=[pl.BlockSpec(memory_space=pltpu.SMEM)] + [vmem] * (len(arrays) + len(pinned)),
        out_specs=[vmem] * len(out_shape),
        out_shape=[jax.ShapeDtypeStruct(shape, jnp.float32) for shape in out_shape],
        cost_estimate=pl.CostEstimate(flops=work[0], bytes_accessed=work[1], transcendentals=0),
        compiler_params=pltpu.CompilerParams(vmem_limit_bytes=8 * 2**20),
    )(scalar.reshape(1), *arrays, *pinned)


def rows_of_both(other_ref, own_ref):
    return jnp.concatenate([other_ref[...], own_ref[...]], 0)


def in_order(y, refs):
    own, two, three, one = [ref[...] for ref in refs]
    blocks = [jnp.where(y == i, own, jnp.where(y == i ^ 1, one, jnp.where(y == i ^ 2, two, three))) for i in range(4)]
    return jnp.concatenate(blocks, 1)


def pack_kernel(y_ref, kept_ref, taken_ref, out_ref):
    rows, width = kept_ref.shape[0], out_ref.shape[1]
    for i in range(kept_ref.shape[1] // width):
        lanes = pl.ds(width * i, width)
        out_ref[rows * i : rows * (i + 1), :] = kept_ref[:, lanes] + taken_ref[:, lanes]


def first_kernel(y_ref, start_ref, sums_ref, other_ref, own_ref, out_ref, own1_ref):
    rows, width = start_ref.shape[0], sums_ref.shape[1]
    blocks = [sums_ref[rows * i : rows * (i + 1), :] for i in range(sums_ref.shape[0] // rows)]
    reduced = start_ref[...] - jnp.concatenate(blocks, 1)
    out_ref[...] = product(reduced, rows_of_both(other_ref, own_ref))
    y, span = y_ref[0], own1_ref.shape[1]
    own1 = reduced[:, :span]
    for i in range(1, reduced.shape[1] // span):
        own1 = jnp.where(y == i, reduced[:, span * i : span * (i + 1)], own1)
    own1_ref[...] = own1


def second_kernel(y_ref, base_ref, own0, two0, three0, one0, other_ref, own_ref, out_ref):
    known = in_order(y_ref[0], (own0, two0, three0, one0))
    out_ref[...] = base_ref[...] - product(known, rows_of_both(other_ref, own_ref))


def third_kernel(y_ref, block0_ref, own1, two1, three1, one1, other_ref, own_ref, out_ref):
    known = in_order(y_ref[0], (own1, two1, three1, one1))
    rows = block0_ref.shape[0]
    out_ref[:rows, :] = block0_ref[...]
    out_ref[rows:, :] = product(known, rows_of_both(other_ref, own_ref))


def unknowns(core_ref, leader_ref, taken_ref):
    return jnp.where(core_ref[0] == 0, taken_ref[...], leader_ref[:, taken_ref.shape[1] :])


def trailing_kernel(own, core_ref, leader_ref, taken_ref, factor_ref, out_ref, *solved_ref):
    solved = unknowns(core_ref, leader_ref, taken_ref)
    if own:
        solved_ref[0][...] = solved
    rhs, width = solved.shape[0] // 2, solved.shape[1]
    count = out_ref.shape[0] // rhs * width
    pad = -rhs % 8
    solved = jnp.concatenate([solved[:rhs], solved[rhs:]], 1)
    solved = jnp.concatenate([solved, jnp.zeros((pad, solved.shape[1]), jnp.float32)], 0)
    head = solved.astype(jnp.bfloat16).astype(jnp.float32)
    both = jnp.concatenate([head, solved - head], 0).astype(jnp.bfloat16)
    head = head.astype(jnp.bfloat16)
    size = count // CHUNKS
    start = pl.multiple_of(2 * count * (core_ref[0] if own else 1 - core_ref[0]), 2 * count)
    for i in range(CHUNKS):
        block = [factor_ref[pl.ds(start + 2 * size * i + k, size, 2), :] for k in range(2)]
        heads, tails = head_and_tail(jnp.concatenate(block, 1))
        main = lax.dot_general(both, heads, NT, preferred_element_type=jnp.float32)
        side = lax.dot_general(head, tails, NT, preferred_element_type=jnp.float32)
        sums = main[:rhs] + (main[rhs + pad : 2 * rhs + pad] + side[:rhs])
        for j in range(size // width):
            first = rhs * (size // width * i + j)
            out_ref[first : first + rhs, :] = sums[:, width * j : width * (j + 1)]


def trailing_products(own, factor, leader, taken, core):
    count, rhs, width = factor.shape[0] // 4, taken.shape[0] // 2, factor.shape[1]
    vmem = pl.BlockSpec(memory_space=pltpu.VMEM)
    out_shape = [jax.ShapeDtypeStruct((count // width * rhs, width), jnp.float32)]
    if own:
        out_shape.append(jax.ShapeDtypeStruct(taken.shape, jnp.float32))
    return pl.pallas_call(
        lambda *refs: trailing_kernel(own, *refs),
        in_specs=[pl.BlockSpec(memory_space=pltpu.SMEM), vmem, vmem, vmem],
        out_specs=[vmem] * len(out_shape),
        out_shape=out_shape,
        cost_estimate=pl.CostEstimate(flops=12 * count * width * rhs, bytes_accessed=8 * count * width, transcendentals=0),
        compiler_params=pltpu.CompilerParams(vmem_limit_bytes=8 * 2**20),
    )(core.reshape(1), leader, taken, pltpu.with_memory_space_constraint(factor, pltpu.VMEM))


def place_kernel(half_ref, value_ref, base_ref, *rest):
    out_ref, held, sem = rest[-3:]
    rhs, count = held.shape
    width = value_ref.shape[1]
    start = pl.multiple_of(half_ref[0] * count, count)
    for j in range(count // width):
        lanes = pl.ds(pl.multiple_of(start + width * j, width), width)
        held[:, width * j : width * (j + 1)] = base_ref[:, lanes] - value_ref[rhs * j : rhs * (j + 1), :]
    copy = pltpu.make_async_copy(held, out_ref.at[:, pl.ds(start, count)], sem)
    copy.start()
    copy.wait()


def place(half, value, base, *target):
    vmem, anywhere = pl.BlockSpec(memory_space=pltpu.VMEM), pl.BlockSpec(memory_space=pl.ANY)
    value, base = (pltpu.with_memory_space_constraint(array, pltpu.VMEM) for array in (value, base))
    return pl.pallas_call(
        place_kernel,
        in_specs=[pl.BlockSpec(memory_space=pltpu.SMEM), vmem, vmem] + [anywhere] * len(target),
        out_specs=anywhere,
        out_shape=jax.ShapeDtypeStruct(base.shape, jnp.float32),
        scratch_shapes=[pltpu.VMEM((base.shape[0], base.shape[1] // 2), jnp.float32), pltpu.SemaphoreType.DMA],
        input_output_aliases={3: 0} if target else {},
        compiler_params=pltpu.CompilerParams(vmem_limit_bytes=8 * 2**20),
    )(half.reshape(1), value, base, *target)


def local(prev_factor, prev_solved, rhs, inverses, coupling, trailing_factor, trailing_rhs):
    width = inverses.shape[1]
    row, col = lax.axis_index("row"), lax.axis_index("col")
    core, y = col & 1, col >> 1
    both = ("row", "col")

    def swap(value, mask0, mask1=None):
        masks = (mask0, mask0 if mask1 is None else mask1)
        return lax.ppermute(value, both, [(i, i ^ masks[i % 2]) for i in range(256)])

    def y_sum(value):
        one, two, three = swap(value, 2, 6), swap(value, 6, 2), swap(value, 4)
        return (three + two) + (one + value)

    def lanes(value, start, size):
        return lax.dynamic_slice_in_dim(value, start, size, value.ndim - 1)

    def by_core(mine, other):
        return jnp.where(core == 0, mine, other), jnp.where(core == 0, other, mine)

    def dot(matrix, value):
        return jnp.einsum("ij,rj->ri", matrix, value, precision=HIGH)

    def among_leaders(value, step, mask):
        return [swap(value, mask, step * i) for i in (2, 3, 1)]

    def from_z(value, source):
        pairs = [(i, i ^ 2) for i in range(0, 256, 2)]
        pairs += [((i & ~56) | source(i >> 3 & 7) << 3, i) for i in range(1, 256, 2)]
        return lax.ppermute(value, both, pairs)

    def z_sum(value):
        value = value + swap(value, 2, 8)
        beside = from_z(value, lambda z: (z + 1 if z & 1 else z - 1) & 7)
        beyond = from_z(value, lambda z: (z - 2 if z & 1 else z + 2) & 7)
        opposite = from_z(value, lambda z: z ^ 5)
        return (value + opposite) + (beyond + beside)

    def here(value):
        return lax.optimization_barrier(jnp.where(core >= 0, value, 0.0))

    given = dot(lax.dynamic_index_in_dim(prev_factor, core, 0, keepdims=False), prev_solved)
    taken = swap(given, 1)
    kept = dot(lax.dynamic_index_in_dim(prev_factor, 1 - core, 0, keepdims=False), prev_solved)
    kept = lax.optimization_barrier(kept)
    rows = prev_solved.shape[0]
    (sums,) = local_call(pack_kernel, [(8 * rows, width)], y, pinned=(kept, taken))
    sums, inverses, coupling, rhs = lax.optimization_barrier((sums, inverses, coupling, rhs))
    other_inverses = swap(inverses, 1)
    inverses0 = here(other_inverses[0]), here(inverses[0])
    inverses1 = here(other_inverses[1]), here(inverses[1])
    one, two, three = swap(sums, 2, 6), swap(sums, 6, 2), swap(sums, 4)
    one, coupling = lax.optimization_barrier((one, coupling))
    couplings = here(swap(coupling, 1)), here(coupling)
    start = jnp.where(row == 0, lax.dynamic_index_in_dim(rhs, 1 - core, 0, keepdims=False), 0.0)
    sums = (three + two) + (one + sums)
    work = (12 * 21 * width * 8 * width, 16 * width * 8 * width)
    shape = (rows, 2 * width)
    block0, own1 = local_call(first_kernel, [shape, shape], y, start, sums, pinned=inverses0, work=work)
    block0, own1 = lax.optimization_barrier((block0, own1))
    others = among_leaders(block0, 2, 64)
    (second,) = local_call(second_kernel, [shape], y, swap(own1, 1), block0, *others, pinned=couplings, work=work)
    others = among_leaders(second, 2, 64)
    (solved,) = local_call(third_kernel, [(2 * rows, 2 * width)], y, block0, second, *others, pinned=inverses1, work=work)
    two, three, one = among_leaders(solved, 64, 2)
    solved = (two + three) + (one + solved)
    solved, trailing_factor = lax.optimization_barrier((solved, trailing_factor))
    solved = z_sum(solved)
    taken = swap(solved[:, :width], 1)

    factor = trailing_factor.reshape(-1, width)
    (other,) = trailing_products(False, factor, solved, taken, core)
    mine, solved = trailing_products(True, factor, solved, taken, core)
    mine = y_sum(mine + swap(other, 1))
    updated = place(1 - core, swap(mine, 1), trailing_rhs, place(core, mine, trailing_rhs))
    return (solved.reshape(2, -1, width), updated)


def solution(mesh):
    in_specs = (
        P(None, None, ("row", "col")),
        P(None, ("row", "col")),
        P(),
        P(None, "col", None),
        P("col", None),
        P("row", None, "col"),
        P(None, "row"),
    )
    out_specs = (P(None, None, "col"), P(None, "row"))
    return jax.shard_map(local, mesh=mesh, in_specs=in_specs, out_specs=out_specs, check_vma=False)
```

```python
import jax
import jax.numpy as jnp
from jax import lax
from jax.experimental import pallas as pl
from jax.experimental.pallas import tpu as pltpu
from jax.sharding import PartitionSpec as P

HIGH = lax.Precision.HIGH
CHUNKS = 2
NT = (((1,), (1,)), ((), ()))


def head_and_tail(value):
    head = value.astype(jnp.bfloat16)
    return head, (value - head.astype(jnp.float32)).astype(jnp.bfloat16)


def product(left, right):
    rows, pad = left.shape[0], -left.shape[0] % 8
    left = jnp.concatenate([left, jnp.zeros((pad, left.shape[1]), jnp.float32)], 0)
    head = left.astype(jnp.bfloat16).astype(jnp.float32)
    both = jnp.concatenate([head, left - head], 0).astype(jnp.bfloat16)
    heads, tails = head_and_tail(right)
    main = lax.dot_general(both, heads, NT, preferred_element_type=jnp.float32)
    side = lax.dot_general(head.astype(jnp.bfloat16), tails, NT, preferred_element_type=jnp.float32)
    return main[:rows] + (main[rows + pad : 2 * rows + pad] + side[:rows])


def local_call(kernel, out_shape, scalar, *arrays, pinned=(), work=(0, 0)):
    vmem = pl.BlockSpec(memory_space=pltpu.VMEM)
    pinned = [pltpu.with_memory_space_constraint(array, pltpu.VMEM) for array in pinned]
    return pl.pallas_call(
        kernel,
        in_specs=[pl.BlockSpec(memory_space=pltpu.SMEM)] + [vmem] * (len(arrays) + len(pinned)),
        out_specs=[vmem] * len(out_shape),
        out_shape=[jax.ShapeDtypeStruct(shape, jnp.float32) for shape in out_shape],
        cost_estimate=pl.CostEstimate(flops=work[0], bytes_accessed=work[1], transcendentals=0),
        compiler_params=pltpu.CompilerParams(vmem_limit_bytes=8 * 2**20),
    )(scalar.reshape(1), *arrays, *pinned)


def rows_of_both(other_ref, own_ref):
    return jnp.concatenate([other_ref[...], own_ref[...]], 0)


def in_order(y, refs):
    own, two, three, one = [ref[...] for ref in refs]
    blocks = [jnp.where(y == i, own, jnp.where(y == i ^ 1, one, jnp.where(y == i ^ 2, two, three))) for i in range(4)]
    return jnp.concatenate(blocks, 1)


def pack_kernel(y_ref, kept_ref, taken_ref, out_ref):
    rows, width = kept_ref.shape[0], out_ref.shape[1]
    for i in range(kept_ref.shape[1] // width):
        lanes = pl.ds(width * i, width)
        out_ref[rows * i : rows * (i + 1), :] = kept_ref[:, lanes] + taken_ref[:, lanes]


def first_kernel(y_ref, start_ref, sums_ref, other_ref, own_ref, out_ref, own1_ref):
    rows, width = start_ref.shape[0], sums_ref.shape[1]
    blocks = [sums_ref[rows * i : rows * (i + 1), :] for i in range(sums_ref.shape[0] // rows)]
    reduced = start_ref[...] - jnp.concatenate(blocks, 1)
    out_ref[...] = product(reduced, rows_of_both(other_ref, own_ref))
    y, span = y_ref[0], own1_ref.shape[1]
    own1 = reduced[:, :span]
    for i in range(1, reduced.shape[1] // span):
        own1 = jnp.where(y == i, reduced[:, span * i : span * (i + 1)], own1)
    own1_ref[...] = own1


def second_kernel(y_ref, base_ref, own0, two0, three0, one0, other_ref, own_ref, out_ref):
    known = in_order(y_ref[0], (own0, two0, three0, one0))
    out_ref[...] = base_ref[...] - product(known, rows_of_both(other_ref, own_ref))


def third_kernel(y_ref, block0_ref, own1, two1, three1, one1, other_ref, own_ref, out_ref):
    known = in_order(y_ref[0], (own1, two1, three1, one1))
    rows = block0_ref.shape[0]
    out_ref[:rows, :] = block0_ref[...]
    out_ref[rows:, :] = product(known, rows_of_both(other_ref, own_ref))


def unknowns(core_ref, leader_ref, taken_ref):
    return jnp.where(core_ref[0] == 0, taken_ref[...], leader_ref[:, taken_ref.shape[1] :])


def trailing_kernel(own, core_ref, leader_ref, taken_ref, factor_ref, out_ref, *solved_ref):
    solved = unknowns(core_ref, leader_ref, taken_ref)
    if own:
        solved_ref[0][...] = solved
    rhs, width = solved.shape[0] // 2, solved.shape[1]
    count = out_ref.shape[0] // rhs * width
    pad = -rhs % 8
    solved = jnp.concatenate([solved[:rhs], solved[rhs:]], 1)
    solved = jnp.concatenate([solved, jnp.zeros((pad, solved.shape[1]), jnp.float32)], 0)
    head = solved.astype(jnp.bfloat16).astype(jnp.float32)
    both = jnp.concatenate([head, solved - head], 0).astype(jnp.bfloat16)
    head = head.astype(jnp.bfloat16)
    size = count // CHUNKS
    start = pl.multiple_of(2 * count * (core_ref[0] if own else 1 - core_ref[0]), 2 * count)
    for i in range(CHUNKS):
        block = [factor_ref[pl.ds(start + 2 * size * i + k, size, 2), :] for k in range(2)]
        heads, tails = head_and_tail(jnp.concatenate(block, 1))
        main = lax.dot_general(both, heads, NT, preferred_element_type=jnp.float32)
        side = lax.dot_general(head, tails, NT, preferred_element_type=jnp.float32)
        sums = main[:rhs] + (main[rhs + pad : 2 * rhs + pad] + side[:rhs])
        for j in range(size // width):
            first = rhs * (size // width * i + j)
            out_ref[first : first + rhs, :] = sums[:, width * j : width * (j + 1)]


def trailing_products(own, factor, leader, taken, core):
    count, rhs, width = factor.shape[0] // 4, taken.shape[0] // 2, factor.shape[1]
    vmem = pl.BlockSpec(memory_space=pltpu.VMEM)
    out_shape = [jax.ShapeDtypeStruct((count // width * rhs, width), jnp.float32)]
    if own:
        out_shape.append(jax.ShapeDtypeStruct(taken.shape, jnp.float32))
    return pl.pallas_call(
        lambda *refs: trailing_kernel(own, *refs),
        in_specs=[pl.BlockSpec(memory_space=pltpu.SMEM), vmem, vmem, vmem],
        out_specs=[vmem] * len(out_shape),
        out_shape=out_shape,
        cost_estimate=pl.CostEstimate(flops=12 * count * width * rhs, bytes_accessed=8 * count * width, transcendentals=0),
        compiler_params=pltpu.CompilerParams(vmem_limit_bytes=8 * 2**20),
    )(core.reshape(1), leader, taken, pltpu.with_memory_space_constraint(factor, pltpu.VMEM))


def place_kernel(half_ref, value_ref, base_ref, *rest):
    out_ref, held, sem = rest[-3:]
    rhs, count = held.shape
    width = value_ref.shape[1]
    start = pl.multiple_of(half_ref[0] * count, count)
    for j in range(count // width):
        lanes = pl.ds(pl.multiple_of(start + width * j, width), width)
        held[:, width * j : width * (j + 1)] = base_ref[:, lanes] - value_ref[rhs * j : rhs * (j + 1), :]
    copy = pltpu.make_async_copy(held, out_ref.at[:, pl.ds(start, count)], sem)
    copy.start()
    copy.wait()


def place(half, value, base, *target):
    vmem, anywhere = pl.BlockSpec(memory_space=pltpu.VMEM), pl.BlockSpec(memory_space=pl.ANY)
    value, base = (pltpu.with_memory_space_constraint(array, pltpu.VMEM) for array in (value, base))
    return pl.pallas_call(
        place_kernel,
        in_specs=[pl.BlockSpec(memory_space=pltpu.SMEM), vmem, vmem] + [anywhere] * len(target),
        out_specs=anywhere,
        out_shape=jax.ShapeDtypeStruct(base.shape, jnp.float32),
        scratch_shapes=[pltpu.VMEM((base.shape[0], base.shape[1] // 2), jnp.float32), pltpu.SemaphoreType.DMA],
        input_output_aliases={3: 0} if target else {},
        compiler_params=pltpu.CompilerParams(vmem_limit_bytes=8 * 2**20),
    )(half.reshape(1), value, base, *target)


def local(prev_factor, prev_solved, rhs, inverses, coupling, trailing_factor, trailing_rhs):
    width = inverses.shape[1]
    row, col = lax.axis_index("row"), lax.axis_index("col")
    core, y = col & 1, col >> 1
    both = ("row", "col")

    def swap(value, mask0, mask1=None):
        masks = (mask0, mask0 if mask1 is None else mask1)
        return lax.ppermute(value, both, [(i, i ^ masks[i % 2]) for i in range(256)])

    def y_sum(value):
        one, two, three = swap(value, 2), swap(value, 6), swap(value, 4)
        return (three + two) + (one + value)

    def lanes(value, start, size):
        return lax.dynamic_slice_in_dim(value, start, size, value.ndim - 1)

    def by_core(mine, other):
        return jnp.where(core == 0, mine, other), jnp.where(core == 0, other, mine)

    def dot(matrix, value):
        return jnp.einsum("ij,rj->ri", matrix, value, precision=HIGH)

    def among_leaders(value, step, mask):
        return [swap(value, mask, step * i) for i in (2, 3, 1)]

    def from_z(value, source):
        pairs = [(i, i ^ 2) for i in range(0, 256, 2)]
        pairs += [((i & ~56) | source(i >> 3 & 7) << 3, i) for i in range(1, 256, 2)]
        return lax.ppermute(value, both, pairs)

    def z_sum(value):
        value = value + swap(value, 2, 8)
        beside = from_z(value, lambda z: (z + 1 if z & 1 else z - 1) & 7)
        beyond = from_z(value, lambda z: (z - 2 if z & 1 else z + 2) & 7)
        opposite = from_z(value, lambda z: z ^ 5)
        return (value + opposite) + (beyond + beside)

    def here(value):
        return lax.optimization_barrier(jnp.where(core >= 0, value, 0.0))

    given = dot(lax.dynamic_index_in_dim(prev_factor, core, 0, keepdims=False), prev_solved)
    taken = swap(given, 1)
    kept = dot(lax.dynamic_index_in_dim(prev_factor, 1 - core, 0, keepdims=False), prev_solved)
    kept = lax.optimization_barrier(kept)
    rows = prev_solved.shape[0]
    (sums,) = local_call(pack_kernel, [(8 * rows, width)], y, pinned=(kept, taken))
    sums, inverses, coupling, rhs = lax.optimization_barrier((sums, inverses, coupling, rhs))
    other_inverses = swap(inverses, 1)
    inverses0 = here(other_inverses[0]), here(inverses[0])
    inverses1 = here(other_inverses[1]), here(inverses[1])
    one, two, three = swap(sums, 2, 6), swap(sums, 6, 2), swap(sums, 4)
    one, coupling = lax.optimization_barrier((one, coupling))
    couplings = here(swap(coupling, 1)), here(coupling)
    start = jnp.where(row == 0, lax.dynamic_index_in_dim(rhs, 1 - core, 0, keepdims=False), 0.0)
    sums = (three + two) + (one + sums)
    work = (12 * 21 * width * 8 * width, 16 * width * 8 * width)
    shape = (rows, 2 * width)
    block0, own1 = local_call(first_kernel, [shape, shape], y, start, sums, pinned=inverses0, work=work)
    block0, own1 = lax.optimization_barrier((block0, own1))
    others = among_leaders(block0, 2, 64)
    (second,) = local_call(second_kernel, [shape], y, swap(own1, 1), block0, *others, pinned=couplings, work=work)
    others = among_leaders(second, 2, 64)
    (solved,) = local_call(third_kernel, [(2 * rows, 2 * width)], y, block0, second, *others, pinned=inverses1, work=work)
    two, three, one = among_leaders(solved, 64, 2)
    solved = (two + three) + (one + solved)
    solved, trailing_factor = lax.optimization_barrier((solved, trailing_factor))
    solved = z_sum(solved)
    taken = swap(solved[:, :width], 1)

    factor = trailing_factor.reshape(-1, width)
    (other,) = trailing_products(False, factor, solved, taken, core)
    mine, solved = trailing_products(True, factor, solved, taken, core)
    mine = y_sum(mine + swap(other, 1))
    updated = place(1 - core, swap(mine, 1), trailing_rhs, place(core, mine, trailing_rhs))
    return (solved.reshape(2, -1, width), updated)


def solution(mesh):
    in_specs = (
        P(None, None, ("row", "col")),
        P(None, ("row", "col")),
        P(),
        P(None, "col", None),
        P("col", None),
        P("row", None, "col"),
        P(None, "row"),
    )
    out_specs = (P(None, None, "col"), P(None, "row"))
    return jax.shard_map(local, mesh=mesh, in_specs=in_specs, out_specs=out_specs, check_vma=False)
```

```python
import jax
import jax.numpy as jnp
from jax import lax
from jax.experimental import pallas as pl
from jax.experimental.pallas import tpu as pltpu
from jax.sharding import PartitionSpec as P

HIGH = lax.Precision.HIGH
CHUNKS = 2
NT = (((1,), (1,)), ((), ()))


def head_and_tail(value):
    head = value.astype(jnp.bfloat16)
    return head, (value - head.astype(jnp.float32)).astype(jnp.bfloat16)


def product(left, right):
    rows, pad = left.shape[0], -left.shape[0] % 8
    left = jnp.concatenate([left, jnp.zeros((pad, left.shape[1]), jnp.float32)], 0)
    head = left.astype(jnp.bfloat16).astype(jnp.float32)
    both = jnp.concatenate([head, left - head], 0).astype(jnp.bfloat16)
    heads, tails = head_and_tail(right)
    main = lax.dot_general(both, heads, NT, preferred_element_type=jnp.float32)
    side = lax.dot_general(head.astype(jnp.bfloat16), tails, NT, preferred_element_type=jnp.float32)
    return main[:rows] + (main[rows + pad : 2 * rows + pad] + side[:rows])


def local_call(kernel, out_shape, scalar, *arrays, pinned=(), work=(0, 0)):
    vmem = pl.BlockSpec(memory_space=pltpu.VMEM)
    pinned = [pltpu.with_memory_space_constraint(array, pltpu.VMEM) for array in pinned]
    return pl.pallas_call(
        kernel,
        in_specs=[pl.BlockSpec(memory_space=pltpu.SMEM)] + [vmem] * (len(arrays) + len(pinned)),
        out_specs=[vmem] * len(out_shape),
        out_shape=[jax.ShapeDtypeStruct(shape, jnp.float32) for shape in out_shape],
        cost_estimate=pl.CostEstimate(flops=work[0], bytes_accessed=work[1], transcendentals=0),
        compiler_params=pltpu.CompilerParams(vmem_limit_bytes=8 * 2**20),
    )(scalar.reshape(1), *arrays, *pinned)


def rows_of_both(other_ref, own_ref):
    return jnp.concatenate([other_ref[...], own_ref[...]], 0)


def in_order(y, refs):
    own, two, three, one = [ref[...] for ref in refs]
    blocks = [jnp.where(y == i, own, jnp.where(y == i ^ 1, one, jnp.where(y == i ^ 2, two, three))) for i in range(4)]
    return jnp.concatenate(blocks, 1)


def pack_kernel(y_ref, kept_ref, taken_ref, out_ref):
    rows, width = kept_ref.shape[0], out_ref.shape[1]
    for i in range(kept_ref.shape[1] // width):
        lanes = pl.ds(width * i, width)
        out_ref[rows * i : rows * (i + 1), :] = kept_ref[:, lanes] + taken_ref[:, lanes]


def first_kernel(y_ref, start_ref, sums_ref, other_ref, own_ref, out_ref, own1_ref):
    rows, width = start_ref.shape[0], sums_ref.shape[1]
    blocks = [sums_ref[rows * i : rows * (i + 1), :] for i in range(sums_ref.shape[0] // rows)]
    reduced = start_ref[...] - jnp.concatenate(blocks, 1)
    out_ref[...] = product(reduced, rows_of_both(other_ref, own_ref))
    y, span = y_ref[0], own1_ref.shape[1]
    own1 = reduced[:, :span]
    for i in range(1, reduced.shape[1] // span):
        own1 = jnp.where(y == i, reduced[:, span * i : span * (i + 1)], own1)
    own1_ref[...] = own1


def second_kernel(y_ref, base_ref, own0, two0, three0, one0, other_ref, own_ref, out_ref):
    known = in_order(y_ref[0], (own0, two0, three0, one0))
    out_ref[...] = base_ref[...] - product(known, rows_of_both(other_ref, own_ref))


def third_kernel(y_ref, block0_ref, own1, two1, three1, one1, other_ref, own_ref, out_ref):
    known = in_order(y_ref[0], (own1, two1, three1, one1))
    rows = block0_ref.shape[0]
    out_ref[:rows, :] = block0_ref[...]
    out_ref[rows:, :] = product(known, rows_of_both(other_ref, own_ref))


def unknowns(core_ref, leader_ref, taken_ref):
    return jnp.where(core_ref[0] == 0, taken_ref[...], leader_ref[:, taken_ref.shape[1] :])


def trailing_kernel(own, core_ref, leader_ref, taken_ref, factor_ref, out_ref, *solved_ref):
    solved = unknowns(core_ref, leader_ref, taken_ref)
    if own:
        solved_ref[0][...] = solved
    rhs, width = solved.shape[0] // 2, solved.shape[1]
    count = out_ref.shape[0] // rhs * width
    pad = -rhs % 8
    solved = jnp.concatenate([solved[:rhs], solved[rhs:]], 1)
    solved = jnp.concatenate([solved, jnp.zeros((pad, solved.shape[1]), jnp.float32)], 0)
    head = solved.astype(jnp.bfloat16).astype(jnp.float32)
    both = jnp.concatenate([head, solved - head], 0).astype(jnp.bfloat16)
    head = head.astype(jnp.bfloat16)
    size = count // CHUNKS
    start = pl.multiple_of(2 * count * (core_ref[0] if own else 1 - core_ref[0]), 2 * count)
    for i in range(CHUNKS):
        block = [factor_ref[pl.ds(start + 2 * size * i + k, size, 2), :] for k in range(2)]
        heads, tails = head_and_tail(jnp.concatenate(block, 1))
        main = lax.dot_general(both, heads, NT, preferred_element_type=jnp.float32)
        side = lax.dot_general(head, tails, NT, preferred_element_type=jnp.float32)
        sums = main[:rhs] + (main[rhs + pad : 2 * rhs + pad] + side[:rhs])
        for j in range(size // width):
            first = rhs * (size // width * i + j)
            out_ref[first : first + rhs, :] = sums[:, width * j : width * (j + 1)]


def trailing_products(own, factor, leader, taken, core):
    count, rhs, width = factor.shape[0] // 4, taken.shape[0] // 2, factor.shape[1]
    vmem = pl.BlockSpec(memory_space=pltpu.VMEM)
    out_shape = [jax.ShapeDtypeStruct((count // width * rhs, width), jnp.float32)]
    if own:
        out_shape.append(jax.ShapeDtypeStruct(taken.shape, jnp.float32))
    return pl.pallas_call(
        lambda *refs: trailing_kernel(own, *refs),
        in_specs=[pl.BlockSpec(memory_space=pltpu.SMEM), vmem, vmem, vmem],
        out_specs=[vmem] * len(out_shape),
        out_shape=out_shape,
        cost_estimate=pl.CostEstimate(flops=12 * count * width * rhs, bytes_accessed=8 * count * width, transcendentals=0),
        compiler_params=pltpu.CompilerParams(vmem_limit_bytes=8 * 2**20),
    )(core.reshape(1), leader, taken, pltpu.with_memory_space_constraint(factor, pltpu.VMEM))


def place_kernel(half_ref, value_ref, base_ref, *rest):
    out_ref, held, sem = rest[-3:]
    rhs, count = held.shape
    width = value_ref.shape[1]
    start = pl.multiple_of(half_ref[0] * count, count)
    for j in range(count // width):
        lanes = pl.ds(pl.multiple_of(start + width * j, width), width)
        held[:, width * j : width * (j + 1)] = base_ref[:, lanes] - value_ref[rhs * j : rhs * (j + 1), :]
    copy = pltpu.make_async_copy(held, out_ref.at[:, pl.ds(start, count)], sem)
    copy.start()
    copy.wait()


def place(half, value, base, *target):
    vmem, anywhere = pl.BlockSpec(memory_space=pltpu.VMEM), pl.BlockSpec(memory_space=pl.ANY)
    value, base = (pltpu.with_memory_space_constraint(array, pltpu.VMEM) for array in (value, base))
    return pl.pallas_call(
        place_kernel,
        in_specs=[pl.BlockSpec(memory_space=pltpu.SMEM), vmem, vmem] + [anywhere] * len(target),
        out_specs=anywhere,
        out_shape=jax.ShapeDtypeStruct(base.shape, jnp.float32),
        scratch_shapes=[pltpu.VMEM((base.shape[0], base.shape[1] // 2), jnp.float32), pltpu.SemaphoreType.DMA],
        input_output_aliases={3: 0} if target else {},
        compiler_params=pltpu.CompilerParams(vmem_limit_bytes=8 * 2**20),
    )(half.reshape(1), value, base, *target)


def local(prev_factor, prev_solved, rhs, inverses, coupling, trailing_factor, trailing_rhs):
    width = inverses.shape[1]
    row, col = lax.axis_index("row"), lax.axis_index("col")
    core, y = col & 1, col >> 1
    both = ("row", "col")

    def swap(value, mask0, mask1=None):
        masks = (mask0, mask0 if mask1 is None else mask1)
        return lax.ppermute(value, both, [(i, i ^ masks[i % 2]) for i in range(256)])

    def y_sum(value):
        one, two, three = swap(value, 2, 6), swap(value, 6, 2), swap(value, 4)
        return (three + two) + (one + value)

    def lanes(value, start, size):
        return lax.dynamic_slice_in_dim(value, start, size, value.ndim - 1)

    def by_core(mine, other):
        return jnp.where(core == 0, mine, other), jnp.where(core == 0, other, mine)

    def dot(matrix, value):
        return jnp.einsum("ij,rj->ri", matrix, value, precision=HIGH)

    def among_leaders(value, step, mask):
        return [swap(value, mask, step * i) for i in (2, 3, 1)]

    def from_z(value, source):
        pairs = [(i, i ^ 2) for i in range(0, 256, 2)]
        pairs += [((i & ~56) | source(i >> 3 & 7) << 3, i) for i in range(1, 256, 2)]
        return lax.ppermute(value, both, pairs)

    def z_sum(value):
        value = value + swap(value, 2, 8)
        beside = from_z(value, lambda z: (z + 1 if z & 1 else z - 1) & 7)
        beyond = from_z(value, lambda z: (z - 2 if z & 1 else z + 2) & 7)
        opposite = from_z(value, lambda z: z ^ 5)
        return (value + opposite) + (beyond + beside)

    def here(value):
        return lax.optimization_barrier(jnp.where(core >= 0, value, 0.0))

    given = dot(lax.dynamic_index_in_dim(prev_factor, core, 0, keepdims=False), prev_solved)
    taken = swap(given, 1)
    kept = dot(lax.dynamic_index_in_dim(prev_factor, 1 - core, 0, keepdims=False), prev_solved)
    kept = lax.optimization_barrier(kept)
    rows = prev_solved.shape[0]
    (sums,) = local_call(pack_kernel, [(8 * rows, width)], y, pinned=(kept, taken))
    sums, inverses, coupling, rhs = lax.optimization_barrier((sums, inverses, coupling, rhs))
    other_inverses = swap(inverses, 1)
    inverses0 = here(other_inverses[0]), here(inverses[0])
    inverses1 = here(other_inverses[1]), here(inverses[1])
    one, two, three = swap(sums, 2, 6), swap(sums, 6, 2), swap(sums, 4)
    three, coupling = lax.optimization_barrier((three, coupling))
    couplings = here(swap(coupling, 1)), here(coupling)
    start = jnp.where(row == 0, lax.dynamic_index_in_dim(rhs, 1 - core, 0, keepdims=False), 0.0)
    sums = (three + two) + (one + sums)
    work = (12 * 21 * width * 8 * width, 16 * width * 8 * width)
    shape = (rows, 2 * width)
    block0, own1 = local_call(first_kernel, [shape, shape], y, start, sums, pinned=inverses0, work=work)
    block0, own1 = lax.optimization_barrier((block0, own1))
    others = among_leaders(block0, 2, 64)
    (second,) = local_call(second_kernel, [shape], y, swap(own1, 1), block0, *others, pinned=couplings, work=work)
    others = among_leaders(second, 2, 64)
    (solved,) = local_call(third_kernel, [(2 * rows, 2 * width)], y, block0, second, *others, pinned=inverses1, work=work)
    two, three, one = among_leaders(solved, 64, 2)
    solved = (two + three) + (one + solved)
    solved, trailing_factor = lax.optimization_barrier((solved, trailing_factor))
    solved = z_sum(solved)
    taken = swap(solved[:, :width], 1)

    factor = trailing_factor.reshape(-1, width)
    (other,) = trailing_products(False, factor, solved, taken, core)
    mine, solved = trailing_products(True, factor, solved, taken, core)
    mine = y_sum(mine + swap(other, 1))
    updated = place(1 - core, swap(mine, 1), trailing_rhs, place(core, mine, trailing_rhs))
    return (solved.reshape(2, -1, width), updated)


def solution(mesh):
    in_specs = (
        P(None, None, ("row", "col")),
        P(None, ("row", "col")),
        P(),
        P(None, "col", None),
        P("col", None),
        P("row", None, "col"),
        P(None, "row"),
    )
    out_specs = (P(None, None, "col"), P(None, "row"))
    return jax.shard_map(local, mesh=mesh, in_specs=in_specs, out_specs=out_specs, check_vma=False)
```
